32 devices in a mesh: parts: 2 (over x), blk: 16 (over z, y, core).
Axes of the slice: x: 2, y: 2, z: 4, core: 2. Of those that a mesh axis runs over, the one named last changes fastest.
Arguments:
- embeddings: bfloat16 [32768, 2048], P(('parts', 'blk')), parts along dimension 0, may hold values from -6 to 6
- projection: bfloat16 [4096, 64], P('parts'), parts along dimension 0, may hold values from -0.125 to 0.125
- loglen: float32 [128], P('parts'), parts along dimension 0, may hold values from 1.6 to 2.6
- left_solves: float32 [24, 32768], P(None, ('parts', 'blk')), parts along dimension 1, may hold values from -0.42426407 to 0.42426407
- right_solves: float32 [24, 32768], P(None, ('parts', 'blk')), parts along dimension 1, may hold values from -0.42426407 to 0.42426407
- assign: int32 [32768], P(('parts', 'blk')), parts along dimension 0, may hold values from 0 to 3
- plan: int32 [4, 32], P(None, ('parts', 'blk')), parts along dimension 1, may hold values from 0 to 65535
Outputs:
- projection_grad: float32 [4096, 64], P('parts'), parts along dimension 0
The draws below stay inside these ranges and needn't reach their ends.
There are 2 independent parts, one for each index of `parts`. The reference program is written for one: setup_inputs(seed, part) draws one part's arguments, and reference() takes and returns one part's arrays. A program takes and returns all parts, laid end to end along the dimension named above; each array names one. Nothing has to cross between parts.
All inputs are finite; a program needn't handle non-finite values.
Results may differ from the reference program's by a relative error of at most 0.0031.
Values sent between devices are 32-bit elements; how exact they have to be, the bound alone decides.
No kernel may reach another device: no remote copies, remote signals or barrier semaphores. Data moves between devices by JAX's collectives and lax.ppermute only.
A program may use at most 128 MiB of HBM per device.

```python
import jax
import jax.numpy as jnp
from jax import lax

E = 2048
F = 64
C = 24
SUB = 4
STEPS = 4
PTS = 1024
NPTS = 16384
N_BLK = 16


def set_ends(array, key, smallest, high):
    index_at = [jax.random.randint(jax.random.fold_in(key, axis), (), 0, length) for axis, length in enumerate(array.shape)]
    longest = array.shape.index(max(array.shape))
    next_to = index_at[:longest] + [(index_at[longest] + 1) % array.shape[longest]] + index_at[longest + 1:]
    return array.at[tuple(index_at)].set(smallest).at[tuple(next_to)].set(high)


def level_of(stream_key, dims, pieces, least, top_value):
    def one(axis_at, parts):
        heights = jax.random.uniform(jax.random.fold_in(jax.random.fold_in(stream_key, 6), axis_at), (parts,), jnp.float32, least / len(pieces), top_value / len(pieces))
        return jnp.repeat(jnp.exp(heights), dims[axis_at] // parts).reshape((-1,) + (1,) * (len(dims) - axis_at - 1))

    gain = one(*pieces[0])
    for cut in pieces[1:]:
        gain = gain * one(*cut)
    return gain


def scatter_about(own_key, dims, width, bound, split=(), kind=jnp.bfloat16):
    array = width * jax.random.normal(own_key, dims, jnp.float32)
    if split:
        array = array * level_of(own_key, dims, split, -0.22, 0.18)
    return jnp.clip(array, -bound, bound).astype(kind)


def setup_inputs(seed: int = 0, part: int = 0) -> dict:
    arg_keys = jax.random.split(jax.random.key(seed), 8)
    part_splits = jax.random.split(jax.random.fold_in(arg_keys[7], part), 8)
    return {
        "embeddings": scatter_about(part_splits[0], (NPTS, E), 1.0, 6.0, ((0, 16),)),
        "projection": scatter_about(part_splits[1], (E, F), E ** -0.5, 0.125),
        "loglen": jnp.clip(jax.random.uniform(part_splits[2], (F,), jnp.float32, 1.6, 2.6), 1.6, 2.6),
        "left_solves": scatter_about(part_splits[3], (C, NPTS), (0.8 * NPTS ** -0.25), 0.42426407, ((1, 16),), jnp.float32),
        "right_solves": scatter_about(part_splits[4], (C, NPTS), (0.8 * NPTS ** -0.25), 0.42426407, ((1, 16),), jnp.float32),
        "assign": set_ends(jax.random.randint(part_splits[5], (NPTS,), 0, SUB), jax.random.fold_in(part_splits[5], 1), 0, SUB - 1).astype(jnp.int32),
        "plan": set_ends(jax.random.randint(part_splits[6], (STEPS, N_BLK), 0, 2 ** (SUB * SUB)), jax.random.fold_in(part_splits[6], 1), 0, (2 ** (SUB * SUB)) - 1).astype(jnp.int32),
    }


HIGH = lax.Precision.HIGHEST

def pair_pattern(pair_bits):
    bit_codes = jnp.arange(SUB * SUB, dtype=jnp.int32).reshape(SUB, SUB)
    return jnp.bitwise_and(jnp.right_shift(pair_bits, bit_codes), 1).astype(jnp.float32)

def split_packet(packet):
    return (packet[:F], packet[F:F + C], packet[F + C:F + 2 * C], packet[F + 2 * C:])

def tile_weights(home, visit, pair_bits, diagonal):
    home_feat, home_left, home_right, home_hot = home
    vis_feat, vis_left, vis_right, vis_hot = visit
    contract = (((0,), (0,)), ((), ()))
    cross = lax.dot_general(home_feat, vis_feat, contract, precision=HIGH)
    home_sq = lax.optimization_barrier(jnp.sum(home_feat * home_feat, axis=0))
    vis_sq = lax.optimization_barrier(jnp.sum(vis_feat * vis_feat, axis=0))
    kernel = jnp.exp(-0.5 * (home_sq[:, None] + vis_sq[None, :] - 2.0 * cross))
    spread = lax.dot_general(home_hot, pair_pattern(pair_bits), contract, precision=HIGH)
    mask = jnp.dot(spread, vis_hot, precision=HIGH)
    coupling = lax.dot_general(home_left, vis_right, contract, precision=HIGH)
    if not diagonal:
        coupling = coupling + lax.dot_general(home_right, vis_left, contract, precision=HIGH)
    return mask * kernel * coupling

def diagonal_grad(home, pair_bits):
    weights = tile_weights(home, home, pair_bits, True)
    sym_weights = weights + weights.T
    features = home[0]
    return -(features * lax.optimization_barrier(jnp.sum(sym_weights, axis=1))[None, :] - jnp.dot(features, sym_weights, precision=HIGH))

def cross_grads(home, visit, pair_bits):
    weights = tile_weights(home, visit, pair_bits, False)
    home_feat = home[0]
    vis_feat = visit[0]
    home_grad = -(home_feat * lax.optimization_barrier(jnp.sum(weights, axis=1))[None, :] - lax.dot_general(vis_feat, weights, (((1,), (1,)), ((), ())), precision=HIGH))
    vis_grad = -(vis_feat * lax.optimization_barrier(jnp.sum(weights, axis=0))[None, :] - jnp.dot(home_feat, weights, precision=HIGH))
    return (home_grad, vis_grad)

def project(embeddings, projection, loglen):
    inverse_len = jnp.exp(-loglen)
    features = lax.dot_general(projection, embeddings, (((0,), (1,)), ((), ())), preferred_element_type=jnp.float32)
    return (features * inverse_len[:, None], inverse_len)

def diagonal_entry(member):
    return diagonal_grad(split_packet(member[0]), member[1])

def cross_entry(member):
    return cross_grads(split_packet(member[0]), split_packet(member[1]), member[2])

def reference(embeddings, projection, loglen, left_solves, right_solves, assign, plan):
    features, inverse_len = project(embeddings, projection, loglen)
    one_hot = (assign[None, :] == jnp.arange(SUB, dtype=jnp.int32)[:, None]).astype(jnp.float32)
    packet = jnp.concatenate([features, left_solves, right_solves, one_hot], axis=0)
    blocks = packet.reshape(packet.shape[0], N_BLK, PTS).transpose(1, 0, 2)
    grad_blocks = lax.map(diagonal_entry, (blocks, plan[0]))
    for offset in range(1, STEPS):
        visiting = jnp.roll(blocks, offset, axis=0)
        home_part, vis_part = lax.map(cross_entry, (blocks, visiting, plan[offset]))
        grad_blocks = grad_blocks + home_part + jnp.roll(vis_part, -offset, axis=0)
    grad_z = grad_blocks.transpose(1, 0, 2).reshape(F, N_BLK * PTS)
    grad_x = (grad_z * inverse_len[:, None]).astype(jnp.bfloat16)
    return lax.dot_general(embeddings, grad_x, (((0,), (1,)), ((), ())), preferred_element_type=jnp.float32)
```

```python
import functools

import jax
import jax.numpy as jnp
from jax import lax
from jax.experimental import pallas as pl
from jax.experimental.pallas import tpu as pltpu
from jax.sharding import PartitionSpec as P

F = 64
C = 24
SUB = 4
STEPS = 4

LEFT = F
RIGHT = F + C
LABEL = F + 2 * C
PLAN = LABEL + 1
CORE = PLAN + STEPS
ROWS = 120

LOG2E = 1.4426950408889634
OFF = -1e30
CHUNK = 256
WIDE = 3 * F
NT = (((1,), (1,)), ((), ()))


def halves(value):
    hi = value.astype(jnp.bfloat16).astype(jnp.float32)
    return hi, value - hi


def thirds(value):
    hi, rest = halves(value)
    mid, low = halves(rest)
    return hi, mid, low


def own_operands(packet):
    points = packet.shape[1]
    z = packet[:F]
    hi, lo = halves(z * LOG2E)
    norm = jnp.sum(z * z, axis=0, keepdims=True) * (-0.5 * LOG2E)
    ones = jnp.ones((1, points), jnp.float32)
    labels = packet[LABEL : LABEL + 1]
    hot = [jnp.where(labels == float(u), 1.0, 0.0) for u in range(SUB)]
    tail = jnp.concatenate(list(thirds(norm)) + [ones] * 3 + hot + [jnp.zeros((54, points), jnp.float32)], axis=0)
    exponent = jnp.concatenate([hi, hi, lo, tail], axis=0)
    lh, ll = halves(packet[LEFT:RIGHT])
    rh, rl = halves(packet[RIGHT:LABEL])
    coupling = jnp.concatenate([lh, lh, ll, rh, rh, rl, jnp.zeros((256 - 6 * C, points), jnp.float32)], axis=0)
    return exponent, coupling


def bias_rows(plan, labels, ahead):
    sub = lax.broadcasted_iota(jnp.int32, (SUB, labels.shape[1]), 0)
    code = jnp.where(ahead, SUB * labels + sub, SUB * sub + labels)
    bit = jnp.bitwise_and(jnp.right_shift(jnp.broadcast_to(plan, code.shape), code), 1)
    return jnp.where(bit == 1, 0.0, OFF)


def visitor_operands(packet, bias, use_left=True, use_right=True):
    points = packet.shape[1]
    z = packet[:F]
    hi, lo = halves(z)
    norm = jnp.sum(z * z, axis=0, keepdims=True) * (-0.5 * LOG2E)
    ones = jnp.ones((1, points), jnp.float32)
    tail = jnp.concatenate([ones] * 3 + list(thirds(norm)) + [bias, jnp.zeros((54, points), jnp.float32)], axis=0)
    exponent = jnp.concatenate([hi, lo, hi, tail], axis=0)
    none = jnp.zeros((3 * C, points), jnp.float32)
    rh, rl = halves(packet[RIGHT:LABEL])
    lh, ll = halves(packet[LEFT:RIGHT])
    with_left = [rh, rl, rh] if use_left else [none]
    with_right = [lh, ll, lh] if use_right else [none]
    coupling = jnp.concatenate(with_left + with_right + [jnp.zeros((256 - 6 * C, points), jnp.float32)], axis=0)
    grads = jnp.concatenate([hi, jnp.ones((F, points), jnp.float32), lo], axis=0)
    return exponent.astype(jnp.bfloat16), coupling.astype(jnp.bfloat16), grads.astype(jnp.bfloat16)


def add_tile(acc_ref, own_exp_ref, own_cpl_ref, exp_ref, cpl_ref, grad_ref):
    points = own_exp_ref.shape[0]

    @pl.loop(0, points // CHUNK)
    def _(step):
        rows = pl.ds(pl.multiple_of(step * CHUNK, CHUNK), CHUNK)
        own_exp = own_exp_ref[rows, :]
        own_cpl = own_cpl_ref[rows, :]
        total = acc_ref[rows, :]
        for part in range(points // CHUNK):
            cols = slice(part * CHUNK, (part + 1) * CHUNK)
            power = jnp.dot(own_exp, exp_ref[:, cols], preferred_element_type=jnp.float32)
            couple = jnp.dot(own_cpl, cpl_ref[:, cols], preferred_element_type=jnp.float32)
            weights = jnp.exp2(power) * couple
            hi = weights.astype(jnp.bfloat16)
            lo = (weights - hi.astype(jnp.float32)).astype(jnp.bfloat16)
            grads = grad_ref[:, cols]
            total = total + lax.dot_general(hi, grads, NT, preferred_element_type=jnp.float32)
            total = total + lax.dot_general(lo, grads, NT, preferred_element_type=jnp.float32)
        acc_ref[rows, :] = total


def visit(packet, plan, ahead, slots, acc_ref, own_exp_ref, own_cpl_ref, **uses):
    exp_ref, cpl_ref, grad_ref = slots
    bias = bias_rows(plan, packet[LABEL : LABEL + 1].astype(jnp.int32), ahead)
    exp_ref[...], cpl_ref[...], grad_ref[...] = visitor_operands(packet, bias, **uses)
    add_tile(acc_ref, own_exp_ref, own_cpl_ref, exp_ref, cpl_ref, grad_ref)


def plan_of(packet, offset):
    return packet[PLAN + offset : PLAN + offset + 1].astype(jnp.int32)


def visit_at(own, packet, ahead, offset_first, offset_second, refs):
    second = own[CORE : CORE + 1] > 0.5
    is_ahead = jnp.where(second, ahead[1], ahead[0]) if ahead[0] != ahead[1] else jnp.full(second.shape, ahead[0])
    mine = jnp.where(second, plan_of(own, offset_second), plan_of(own, offset_first))
    theirs = jnp.where(second, plan_of(packet, offset_second), plan_of(packet, offset_first))
    plan = jnp.where(is_ahead, theirs, mine)
    acc_ref, own_exp_ref, own_cpl_ref, slots = refs
    visit(packet, plan, is_ahead, slots, acc_ref, own_exp_ref, own_cpl_ref)


def home_kernel(own_ref, acc_ref, own_exp_ref, own_cpl_ref, *slots):
    own = own_ref[...]
    exponent, coupling = own_operands(own)
    own_exp_ref[...] = exponent.T.astype(jnp.bfloat16)
    own_cpl_ref[...] = coupling.T.astype(jnp.bfloat16)
    acc_ref[...] = jnp.zeros_like(acc_ref)
    plan = plan_of(own, 0)
    behind = jnp.zeros(plan.shape, jnp.bool_)
    visit(own, plan, behind, slots, acc_ref, own_exp_ref, own_cpl_ref, use_right=False)
    visit(own, plan, ~behind, slots, acc_ref, own_exp_ref, own_cpl_ref, use_left=False)


def visit_kernel(places, *refs):
    n = len(places)
    own_ref, own_exp_ref, own_cpl_ref, before_ref = refs[:4]
    packets, acc_ref, slots = refs[4 : 4 + n], refs[4 + n], refs[5 + n :]
    acc_ref[...] = before_ref[...]
    own = own_ref[...]
    for packet_ref, (ahead, first, second) in zip(packets, places):
        visit_at(own, packet_ref[...], ahead, first, second, (acc_ref, own_exp_ref, own_cpl_ref, slots))


def slots_of(points):
    return [
        pltpu.VMEM((256, points), jnp.bfloat16),
        pltpu.VMEM((256, points), jnp.bfloat16),
        pltpu.VMEM((WIDE, points), jnp.bfloat16),
    ]


def cost(points, tiles):
    return pl.CostEstimate(
        flops=tiles * 8 * points * points * 256, bytes_accessed=1 << 20, transcendentals=tiles * points * points
    )


PARAMS = pltpu.CompilerParams(vmem_limit_bytes=40 << 20)


def home_tile(packet):
    points = packet.shape[1]
    return pl.pallas_call(
        home_kernel,
        out_shape=(
            jax.ShapeDtypeStruct((points, WIDE), jnp.float32),
            jax.ShapeDtypeStruct((points, 256), jnp.bfloat16),
            jax.ShapeDtypeStruct((points, 256), jnp.bfloat16),
        ),
        scratch_shapes=slots_of(points),
        cost_estimate=cost(points, 2),
        compiler_params=PARAMS,
        name="home_tile",
    )(packet)


def visitor_tiles(own, own_exp, own_cpl, acc, packets, places):
    points = own.shape[1]
    return pl.pallas_call(
        functools.partial(visit_kernel, places),
        out_shape=jax.ShapeDtypeStruct(acc.shape, jnp.float32),
        scratch_shapes=slots_of(points),
        cost_estimate=cost(points, len(places)),
        compiler_params=PARAMS,
        name="visitor_tiles",
    )(own, own_exp, own_cpl, acc, *packets)


def sent(value, target):
    count = lax.axis_size("blk")
    return lax.ppermute(value, "blk", [(source, target(source) % count) for source in range(count)])


def twin(value):
    return sent(value, lambda i: i ^ 1)


def sum_over_blk(term):
    count = lax.axis_size("blk")
    index = lax.axis_index("blk")
    second = (index % 2) == 1
    half = term.shape[0] // 2
    give = jnp.where(second, term[:half], term[half:])
    total = jnp.where(second, term[half:], term[:half]) + twin(give)
    spreads, unit = [], 4
    while unit < count:
        spread = min(4, count // unit)
        place = (index // unit) % spread
        if total.shape[0] % spread == 0:
            spreads.append((unit, spread, place))
            shares = total.reshape(spread, total.shape[0] // spread, total.shape[1])
            total = lax.dynamic_index_in_dim(shares, place, 0, False)
            for hop in range(spread - 1, 0, -1):
                passed = lax.dynamic_index_in_dim(shares, place ^ hop, 0, False)
                total = total + sent(passed, lambda i, step=unit * hop: i ^ step)
        else:
            for bit in range(1, spread.bit_length()):
                total = total + sent(total, lambda i, step=unit * bit: i ^ step)
        unit *= spread
    total = total + sent(total, lambda i: i ^ 2)
    for unit, spread, place in reversed(spreads):
        got = [total] + [sent(total, lambda i, step=unit * hop: i ^ step) for hop in range(1, spread)]
        got = jnp.stack(got)
        total = jnp.concatenate([lax.dynamic_index_in_dim(got, place ^ at, 0, False) for at in range(spread)])
    other = twin(total)
    return jnp.where(second, jnp.concatenate([other, total]), jnp.concatenate([total, other]))


def project(embeddings, projection, loglen):
    inverse_len = jnp.exp(-loglen)
    features = lax.dot_general(
        projection, embeddings, (((0,), (1,)), ((), ())), preferred_element_type=jnp.float32
    )
    return (features * inverse_len[:, None], inverse_len)


def per_device(embeddings, projection, loglen, left_solves, right_solves, assign, plan):
    points = embeddings.shape[0]
    features, inverse_len = project(embeddings, projection, loglen)
    core = lax.axis_index("blk") % 2
    rest = jnp.concatenate(
        [
            assign[None, :].astype(jnp.float32),
            jnp.broadcast_to(plan.astype(jnp.float32), (STEPS, points)),
            jnp.broadcast_to(core.astype(jnp.float32), (1, points)),
            jnp.zeros((ROWS - CORE - 1, points), jnp.float32),
        ],
        axis=0,
    )
    own = jnp.concatenate([features, left_solves, right_solves, rest], axis=0)
    near = twin(own)
    down = sent(own, lambda i: i + 2)
    up = sent(own, lambda i: i - 2)
    far = sent(own, lambda i: i + 3 if i % 2 else i - 3)
    acc, own_exp, own_cpl = home_tile(own)
    tiles = functools.partial(visitor_tiles, own, own_exp, own_cpl)
    acc = tiles(acc, [near], [((True, False), 1, 1)])
    acc = tiles(acc, [down, twin(down)], [((False, False), 2, 2), ((False, False), 1, 3)])
    acc = tiles(acc, [far], [((False, True), 3, 3)])
    acc = tiles(acc, [up, twin(up)], [((True, True), 2, 2), ((True, True), 3, 1)])
    grad_z = (acc[:, :F] + acc[:, 2 * F :]).T - features * acc[:, F : 2 * F].T
    grad_x = (grad_z * inverse_len[:, None]).astype(jnp.bfloat16)
    local_term = lax.dot_general(
        grad_x, embeddings, (((1,), (0,)), ((), ())), preferred_element_type=jnp.float32
    )
    return sum_over_blk(local_term).T


def solution(mesh):
    return jax.shard_map(
        per_device,
        mesh=mesh,
        in_specs=(
            P(("parts", "blk"), None),
            P("parts", None),
            P("parts"),
            P(None, ("parts", "blk")),
            P(None, ("parts", "blk")),
            P(("parts", "blk")),
            P(None, ("parts", "blk")),
        ),
        out_specs=P("parts", None),
        check_vma=False,
    )
```

```python
import functools

import jax
import jax.numpy as jnp
from jax import lax
from jax.experimental import pallas as pl
from jax.experimental.pallas import tpu as pltpu
from jax.sharding import PartitionSpec as P

F = 64
C = 24
SUB = 4
STEPS = 4

LEFT = F
RIGHT = F + C
LABEL = F + 2 * C
PLAN = LABEL + 1
CORE = PLAN + STEPS
ROWS = 120

LOG2E = 1.4426950408889634
OFF = -1e30
CHUNK = 512
PIECES = 8
WIDE = 3 * F
FAR = ((False, 3), (True, 3))
NT = (((1,), (1,)), ((), ()))


def halves(value):
    hi = value.astype(jnp.bfloat16).astype(jnp.float32)
    return hi, value - hi


def thirds(value):
    hi, rest = halves(value)
    mid, low = halves(rest)
    return hi, mid, low


def own_operands(packet):
    points = packet.shape[1]
    z = packet[:F]
    hi, lo = halves(z * LOG2E)
    norm = jnp.sum(z * z, axis=0, keepdims=True) * (-0.5 * LOG2E)
    ones = jnp.ones((1, points), jnp.float32)
    labels = packet[LABEL : LABEL + 1]
    hot = [jnp.where(labels == float(u), 1.0, 0.0) for u in range(SUB)]
    tail = jnp.concatenate(list(thirds(norm)) + [ones] * 3 + hot + [jnp.zeros((54, points), jnp.float32)], axis=0)
    exponent = jnp.concatenate([hi, hi, lo, tail], axis=0)
    lh, ll = halves(packet[LEFT:RIGHT])
    rh, rl = halves(packet[RIGHT:LABEL])
    coupling = jnp.concatenate([lh, lh, ll, rh, rh, rl, jnp.zeros((256 - 6 * C, points), jnp.float32)], axis=0)
    return exponent, coupling


def bias_rows(plan, labels, ahead):
    sub = lax.broadcasted_iota(jnp.int32, (SUB, labels.shape[1]), 0)
    code = jnp.where(ahead, SUB * labels + sub, SUB * sub + labels)
    bit = jnp.bitwise_and(jnp.right_shift(jnp.broadcast_to(plan, code.shape), code), 1)
    return jnp.where(bit == 1, 0.0, OFF)


def gradient_rows(hi, lo):
    return jnp.concatenate([hi, jnp.ones_like(hi), lo], axis=0)


def visitor_operands(packet, bias, use_left=True, use_right=True):
    points = packet.shape[1]
    z = packet[:F]
    hi, lo = halves(z)
    norm = jnp.sum(z * z, axis=0, keepdims=True) * (-0.5 * LOG2E)
    ones = jnp.ones((1, points), jnp.float32)
    tail = jnp.concatenate([ones] * 3 + list(thirds(norm)) + [bias, jnp.zeros((54, points), jnp.float32)], axis=0)
    exponent = jnp.concatenate([hi, lo, hi, tail], axis=0)
    none = jnp.zeros((3 * C, points), jnp.float32)
    rh, rl = halves(packet[RIGHT:LABEL])
    lh, ll = halves(packet[LEFT:RIGHT])
    with_left = [rh, rl, rh] if use_left else [none]
    with_right = [lh, ll, lh] if use_right else [none]
    coupling = jnp.concatenate(with_left + with_right + [jnp.zeros((256 - 6 * C, points), jnp.float32)], axis=0)
    grads = gradient_rows(hi, lo)
    return exponent.astype(jnp.bfloat16), coupling.astype(jnp.bfloat16), grads.astype(jnp.bfloat16)


def add_tile(acc_ref, before_ref, home_exp_ref, home_cpl_ref, slots, back=None):
    exp_ref, cpl_ref, grad_ref = slots
    points, visitors = home_exp_ref.shape[0], exp_ref.shape[1]
    for row in range(0, points, CHUNK):
        rows = slice(row, row + CHUNK)
        home_exp, home_cpl = home_exp_ref[rows, :], home_cpl_ref[rows, :]
        total = None if before_ref is None else before_ref[rows, :]
        for col in range(0, visitors, CHUNK):
            cols = slice(col, col + CHUNK)
            power = jnp.dot(home_exp, exp_ref[:, cols], preferred_element_type=jnp.float32)
            couple = jnp.dot(home_cpl, cpl_ref[:, cols], preferred_element_type=jnp.float32)
            weights = jnp.exp2(power) * couple
            hi = weights.astype(jnp.bfloat16)
            lo = (weights - hi.astype(jnp.float32)).astype(jnp.bfloat16)
            for part in (hi, lo):
                term = lax.dot_general(part, grad_ref[:, cols], NT, preferred_element_type=jnp.float32)
                total = term if total is None else total + term
            if back is not None:
                back_ref, home_rows_ref, fresh = back
                term = jnp.dot(home_rows_ref[:, rows], hi, preferred_element_type=jnp.float32)
                term += jnp.dot(home_rows_ref[:, rows], lo, preferred_element_type=jnp.float32)
                back_ref[:, cols] = term if fresh and row == 0 else back_ref[:, cols] + term
        acc_ref[rows, :] = total


def visit(packet, plan, ahead, slots, acc_ref, before_ref, home_exp_ref, home_cpl_ref, back=None, **uses):
    exp_ref, cpl_ref, grad_ref = slots
    bias = bias_rows(plan, packet[LABEL : LABEL + 1].astype(jnp.int32), ahead)
    exp_ref[...], cpl_ref[...], grad_ref[...] = visitor_operands(packet, bias, **uses)
    add_tile(acc_ref, before_ref, home_exp_ref, home_cpl_ref, slots, back)


def plan_of(packet, offset):
    return packet[PLAN + offset : PLAN + offset + 1].astype(jnp.int32)


def visit_at(second, home, packet, place, acc_ref, before_ref, factors, slots, back=None):
    (ahead_first, offset_first), (ahead_second, offset_second) = place
    ahead = jnp.logical_or(jnp.logical_and(second, ahead_second), jnp.logical_and(~second, ahead_first))
    mine = jnp.where(second, plan_of(home, offset_second), plan_of(home, offset_first))
    theirs = jnp.where(second, plan_of(packet, offset_second), plan_of(packet, offset_first))
    plan = jnp.where(ahead, theirs, mine)
    visit(packet, plan, ahead, slots, acc_ref, before_ref, *factors, back=back)


def prepare(packet, exp_ref, cpl_ref, rows_ref):
    exponent, coupling = own_operands(packet)
    exp_ref[...] = exponent.T.astype(jnp.bfloat16)
    cpl_ref[...] = coupling.T.astype(jnp.bfloat16)
    rows_ref[...] = gradient_rows(*halves(packet[:F])).astype(jnp.bfloat16)


def is_second(own_ref):
    return own_ref[CORE : CORE + 1, :] > 0.5


def home_kernel(own_ref, acc_ref, exp_ref, cpl_ref, rows_ref, again_ref, *slots):
    own = own_ref[...]
    again_ref[...] = own
    prepare(own, exp_ref, cpl_ref, rows_ref)
    plan = plan_of(own, 0)
    behind = jnp.zeros(plan.shape, jnp.bool_)
    visit(own, plan, behind, slots, acc_ref, None, exp_ref, cpl_ref, use_right=False)
    visit(own, plan, ~behind, slots, acc_ref, acc_ref, exp_ref, cpl_ref, use_left=False)


def near_kernel(own_ref, exp_ref, cpl_ref, before_ref, near_ref, acc_ref, near_exp_ref, near_cpl_ref, near_rows_ref, *slots):
    near = near_ref[...]
    prepare(near, near_exp_ref, near_cpl_ref, near_rows_ref)
    place = ((True, 1), (False, 1))
    visit_at(is_second(own_ref), own_ref[...], near, place, acc_ref, before_ref, (exp_ref, cpl_ref), slots)


def gradient(sums, packet_ref):
    return sums[:F] + sums[2 * F :] - packet_ref[:F, :] * sums[F : 2 * F]


def down_kernel(*refs):
    own_ref, exp_ref, cpl_ref, rows_ref, before_ref, near_ref, near_exp_ref, near_cpl_ref, near_rows_ref, down_ref = refs[:10]
    acc_ref, near_grad_ref, back_grad_ref, near_acc_ref, back_ref, *slots = refs[10:]
    second, down = is_second(own_ref), down_ref[...]
    place = ((False, 3), (False, 1))
    back = (back_ref, near_rows_ref, True)
    visit_at(second, near_ref[...], down, place, near_acc_ref, None, (near_exp_ref, near_cpl_ref), slots, back)
    near_grad_ref[...] = gradient(near_acc_ref[...].T, near_ref)
    place = ((False, 2), (False, 2))
    back = (back_ref, rows_ref, False)
    visit_at(second, own_ref[...], down, place, acc_ref, before_ref, (exp_ref, cpl_ref), slots, back)
    back_grad_ref[...] = gradient(back_ref[...], down_ref)


def far_kernel(own_ref, exp_ref, cpl_ref, before_ref, far_ref, more_far_ref, passed_ref, embeddings_ref, grad_ref, acc_ref, *slots):
    far = far_ref[...] + more_far_ref[...]
    visit_at(is_second(own_ref), own_ref[...], far, FAR, acc_ref, before_ref, (exp_ref, cpl_ref), slots)
    grad_ref[...] = gradient(acc_ref[...].T, own_ref) + passed_ref[...]


def last_kernel(grad_ref, back_ref, loglen_ref, embeddings_ref, term_ref):
    grad_z = grad_ref[...] + back_ref[...]
    grad_x = (grad_z * as_column(jnp.exp(-loglen_ref[...]))).astype(jnp.bfloat16)
    for col in range(0, term_ref.shape[1], 512):
        cols = slice(col, col + 512)
        term_ref[:, cols] = jnp.dot(grad_x, embeddings_ref[:, cols], preferred_element_type=jnp.float32)


def as_column(row):
    n = row.shape[1]
    same = lax.broadcasted_iota(jnp.int32, (n, n), 0) == lax.broadcasted_iota(jnp.int32, (n, n), 1)
    return jnp.sum(jnp.where(same, jnp.broadcast_to(row, (n, n)), 0.0), axis=1, keepdims=True)


def project_kernel(plan_ref, projection_ref, loglen_ref, assign_ref, left_ref, right_ref, embeddings_ref, own_ref, *scratch):
    held, sems = scratch[:6], scratch[6]
    points = own_ref.shape[1]
    block = points // PIECES
    sources = (projection_ref, loglen_ref, assign_ref, left_ref, right_ref)
    copies = [pltpu.make_async_copy(source, there, sems.at[n]) for n, (source, there) in enumerate(zip(sources, held))]
    for piece in range(PIECES):
        rows = pl.ds(piece * block, block)
        copies.append(pltpu.make_async_copy(embeddings_ref.at[rows, :], held[5].at[rows, :], sems.at[5 + piece]))
    for copy in copies:
        copy.start()
    for copy in copies[:5]:
        copy.wait()
    projection, loglen, assign, left, right = (there[...] for there in held[:5])
    core = lax.rem(lax.axis_index("blk"), 2).astype(jnp.float32)
    own_ref[LEFT:RIGHT, :] = left
    own_ref[RIGHT:LABEL, :] = right
    rows = [assign.astype(jnp.float32)]
    rows += [jnp.full((1, points), plan_ref[0, offset].astype(jnp.float32)) for offset in range(STEPS)]
    rows += [jnp.full((1, points), core), jnp.zeros((ROWS - CORE - 1, points), jnp.float32)]
    own_ref[LABEL:, :] = jnp.concatenate(rows, axis=0)
    scale = as_column(jnp.exp(-loglen))
    for piece in range(PIECES):
        copies[5 + piece].wait()
        at = slice(piece * block, (piece + 1) * block)
        features = lax.dot_general(held[5][at, :], projection, NT, preferred_element_type=jnp.float32)
        own_ref[:F, at] = features.T * scale


def slots_of(points):
    return [
        pltpu.VMEM((256, points), jnp.bfloat16),
        pltpu.VMEM((256, points), jnp.bfloat16),
        pltpu.VMEM((WIDE, points), jnp.bfloat16),
    ]


def cost(flops, size=4 << 20):
    return pl.CostEstimate(flops=flops, bytes_accessed=size, transcendentals=0)


def project(embeddings, projection, loglen, left_solves, right_solves, assign, plan):
    points = embeddings.shape[0]
    arrays = (projection.T, loglen[None, :], assign[None, :], left_solves, right_solves, embeddings)
    return pl.pallas_call(
        project_kernel,
        in_specs=[pl.BlockSpec(memory_space=pltpu.SMEM)] + [pl.BlockSpec(memory_space=pltpu.HBM)] * len(arrays),
        out_shape=jax.ShapeDtypeStruct((ROWS, points), jnp.float32),
        scratch_shapes=[pltpu.VMEM(array.shape, array.dtype) for array in arrays]
        + [pltpu.SemaphoreType.DMA((5 + PIECES,))],
        cost_estimate=cost(1 << 20),
        compiler_params=pltpu.CompilerParams(vmem_limit_bytes=62 << 20),
        name="project",
    )(plan.T, *arrays)


def tiles(kernel, outs, points, *operands, scratch=()):
    return pl.pallas_call(
        kernel,
        out_shape=outs,
        scratch_shapes=list(scratch) + (slots_of(points) if points else []),
        cost_estimate=cost(1 << 20),
        compiler_params=pltpu.CompilerParams(vmem_limit_bytes=40 << 20),
        name=kernel.__name__,
    )(*operands)


def sent(value, target, takes=lambda source: True):
    count = lax.axis_size("blk")
    pairs = [(source, target(source) % count) for source in range(count) if takes(source)]
    return lax.ppermute(value, "blk", pairs)


def twin(value):
    return sent(value, lambda i: i ^ 1)


def sum_over_blk(term):
    count = lax.axis_size("blk")
    index = lax.axis_index("blk")
    second = (index % 2) == 1
    half = term.shape[0] // 2
    give = jnp.where(second, term[:half], term[half:])
    total = jnp.where(second, term[half:], term[:half]) + twin(give)
    spreads, unit = [], 4
    while unit < count:
        spread = min(4, count // unit)
        place = (index // unit) % spread
        if total.shape[0] % spread == 0:
            spreads.append((unit, spread, place))
            shares = total.reshape(spread, total.shape[0] // spread, total.shape[1])
            total = lax.dynamic_index_in_dim(shares, place, 0, False)
            for hop in range(spread - 1, 0, -1):
                passed = lax.dynamic_index_in_dim(shares, place ^ hop, 0, False)
                total = total + sent(passed, lambda i, step=unit * hop: i ^ step)
        else:
            for bit in range(1, spread.bit_length()):
                total = total + sent(total, lambda i, step=unit * bit: i ^ step)
        unit *= spread
    total = total + sent(total, lambda i: i ^ 2)
    for unit, spread, place in reversed(spreads):
        got = [total] + [sent(total, lambda i, step=unit * hop: i ^ step) for hop in range(1, spread)]
        got = jnp.stack(got)
        total = jnp.concatenate([lax.dynamic_index_in_dim(got, place ^ at, 0, False) for at in range(spread)])
    other = twin(total)
    return jnp.where(second, jnp.concatenate([other, total]), jnp.concatenate([total, other]))


def across(i):
    return i + 3 if i % 2 else i - 3


def per_device(embeddings, projection, loglen, left_solves, right_solves, assign, plan):
    points, width = embeddings.shape
    sums = jax.ShapeDtypeStruct((points, WIDE), jnp.float32)
    factor = jax.ShapeDtypeStruct((points, 256), jnp.bfloat16)
    rows = jax.ShapeDtypeStruct((WIDE, points), jnp.bfloat16)
    block = jax.ShapeDtypeStruct((ROWS, points), jnp.float32)
    grads = jax.ShapeDtypeStruct((F, points), jnp.float32)
    sums_held = pltpu.VMEM(sums.shape, sums.dtype)

    own = project(embeddings, projection, loglen, left_solves, right_solves, assign, plan)
    down = sent(own, lambda i: i + 2)
    far_odd = sent(own, across, lambda i: i // 2 % 2 == 1)
    near = twin(own)
    acc, own_exp, own_cpl, own_rows, own = tiles(home_kernel, (sums, factor, factor, rows, block), points, own)
    far_even = sent(own, across, lambda i: i // 2 % 2 == 0)
    home = (own, own_exp, own_cpl)
    acc, *near_factors = tiles(near_kernel, (sums, factor, factor, rows), points, *home, acc, near)
    acc, near_grad, down_grad = tiles(
        down_kernel,
        (sums, grads, grads),
        points,
        *home,
        own_rows,
        acc,
        near,
        *near_factors,
        down,
        scratch=[sums_held, pltpu.VMEM((WIDE, points), jnp.float32)],
    )
    passed = twin(near_grad)
    back = sent(down_grad, lambda i: i - 2)
    grad = tiles(far_kernel, grads, points, *home, acc, far_odd, far_even, passed, embeddings, scratch=[sums_held])
    term = tiles(
        last_kernel, jax.ShapeDtypeStruct((F, width), jnp.float32), None, grad, back, loglen[None, :], embeddings
    )
    return sum_over_blk(term).T


def solution(mesh):
    return jax.shard_map(
        per_device,
        mesh=mesh,
        in_specs=(
            P(("parts", "blk"), None),
            P("parts", None),
            P("parts"),
            P(None, ("parts", "blk")),
            P(None, ("parts", "blk")),
            P(("parts", "blk")),
            P(None, ("parts", "blk")),
        ),
        out_specs=P("parts", None),
        check_vma=False,
    )
```

```python
import functools

import jax
import jax.numpy as jnp
from jax import lax
from jax.experimental import pallas as pl
from jax.experimental.pallas import tpu as pltpu
from jax.sharding import PartitionSpec as P

F = 64
C = 24
SUB = 4
STEPS = 4

LEFT = F
RIGHT = F + C
LABEL = F + 2 * C
PLAN = LABEL + 1
CORE = PLAN + STEPS
ROWS = 120

LOG2E = 1.4426950408889634
OFF = -1e30
CHUNK = 512
PIECES = 2
WIDE = 3 * F
FAR = ((False, 3), (True, 3))
NT = (((1,), (1,)), ((), ()))


def halves(value):
    hi = value.astype(jnp.bfloat16).astype(jnp.float32)
    return hi, value - hi


def thirds(value):
    hi, rest = halves(value)
    mid, low = halves(rest)
    return hi, mid, low


def own_operands(packet):
    points = packet.shape[1]
    z = packet[:F]
    hi, lo = halves(z * LOG2E)
    norm = jnp.sum(z * z, axis=0, keepdims=True) * (-0.5 * LOG2E)
    ones = jnp.ones((1, points), jnp.float32)
    labels = packet[LABEL : LABEL + 1]
    hot = [jnp.where(labels == float(u), 1.0, 0.0) for u in range(SUB)]
    tail = jnp.concatenate(list(thirds(norm)) + [ones] * 3 + hot + [jnp.zeros((54, points), jnp.float32)], axis=0)
    exponent = jnp.concatenate([hi, hi, lo, tail], axis=0)
    lh, ll = halves(packet[LEFT:RIGHT])
    rh, rl = halves(packet[RIGHT:LABEL])
    coupling = jnp.concatenate([lh, lh, ll, rh, rh, rl, jnp.zeros((256 - 6 * C, points), jnp.float32)], axis=0)
    return exponent, coupling


def bias_rows(plan, labels, ahead):
    sub = lax.broadcasted_iota(jnp.int32, (SUB, labels.shape[1]), 0)
    code = jnp.where(ahead, SUB * labels + sub, SUB * sub + labels)
    bit = jnp.bitwise_and(jnp.right_shift(jnp.broadcast_to(plan, code.shape), code), 1)
    return jnp.where(bit == 1, 0.0, OFF)


def gradient_rows(hi, lo):
    return jnp.concatenate([hi, jnp.ones_like(hi), lo], axis=0)


def visitor_operands(packet, bias, use_left=True, use_right=True):
    points = packet.shape[1]
    z = packet[:F]
    hi, lo = halves(z)
    norm = jnp.sum(z * z, axis=0, keepdims=True) * (-0.5 * LOG2E)
    ones = jnp.ones((1, points), jnp.float32)
    tail = jnp.concatenate([ones] * 3 + list(thirds(norm)) + [bias, jnp.zeros((54, points), jnp.float32)], axis=0)
    exponent = jnp.concatenate([hi, lo, hi, tail], axis=0)
    none = jnp.zeros((3 * C, points), jnp.float32)
    rh, rl = halves(packet[RIGHT:LABEL])
    lh, ll = halves(packet[LEFT:RIGHT])
    with_left = [rh, rl, rh] if use_left else [none]
    with_right = [lh, ll, lh] if use_right else [none]
    coupling = jnp.concatenate(with_left + with_right + [jnp.zeros((256 - 6 * C, points), jnp.float32)], axis=0)
    grads = gradient_rows(hi, lo)
    return exponent.astype(jnp.bfloat16), coupling.astype(jnp.bfloat16), grads.astype(jnp.bfloat16)


def weights_of(home_exp, home_cpl, exp_ref, cpl_ref, cols):
    power = jnp.dot(home_exp, exp_ref[:, cols], preferred_element_type=jnp.float32)
    couple = jnp.dot(home_cpl, cpl_ref[:, cols], preferred_element_type=jnp.float32)
    weights = jnp.exp2(power) * couple
    hi = weights.astype(jnp.bfloat16)
    return hi, (weights - hi.astype(jnp.float32)).astype(jnp.bfloat16)


def add_tile(acc_ref, before_ref, home_exp_ref, home_cpl_ref, exp_ref, cpl_ref, grad_ref):
    points, visitors = home_exp_ref.shape[0], exp_ref.shape[1]
    for row in range(0, points, CHUNK):
        rows = slice(row, row + CHUNK)
        home_exp, home_cpl = home_exp_ref[rows, :], home_cpl_ref[rows, :]
        total = None if before_ref is None else before_ref[rows, :]
        for col in range(0, visitors, CHUNK):
            cols = slice(col, col + CHUNK)
            for part in weights_of(home_exp, home_cpl, exp_ref, cpl_ref, cols):
                term = lax.dot_general(part, grad_ref[:, cols], NT, preferred_element_type=jnp.float32)
                total = term if total is None else total + term
        acc_ref[rows, :] = total


def back_tile(back_ref, fresh, home_exp_ref, home_cpl_ref, home_rows_ref, exp_ref, cpl_ref, hi_ref, lo_ref):
    points, visitors = home_exp_ref.shape[0], exp_ref.shape[1]
    for row in range(0, points, CHUNK):
        rows = slice(row, row + CHUNK)
        home_exp, home_cpl, home_rows = home_exp_ref[rows, :], home_cpl_ref[rows, :], home_rows_ref[:, rows]
        for col in range(0, visitors, CHUNK):
            cols = slice(col, col + CHUNK)
            hi, lo = weights_of(home_exp, home_cpl, exp_ref, cpl_ref, cols)
            hi_ref[rows, cols], lo_ref[rows, cols] = hi, lo
            term = jnp.dot(home_rows, hi, preferred_element_type=jnp.float32)
            term += jnp.dot(home_rows, lo, preferred_element_type=jnp.float32)
            back_ref[:, cols] = term if fresh and row == 0 else back_ref[:, cols] + term


def side_tile(acc_ref, before_ref, hi_ref, lo_ref, grad_ref):
    points, visitors = hi_ref.shape
    for row in range(0, points, CHUNK):
        rows = slice(row, row + CHUNK)
        total = None if before_ref is None else before_ref[rows, :]
        for col in range(0, visitors, CHUNK):
            cols = slice(col, col + CHUNK)
            for part in (hi_ref[rows, cols], lo_ref[rows, cols]):
                term = lax.dot_general(part, grad_ref[:, cols], NT, preferred_element_type=jnp.float32)
                total = term if total is None else total + term
        acc_ref[rows, :] = total


def load(slots, packet, plan, ahead, **uses):
    exp_ref, cpl_ref, grad_ref = slots
    bias = bias_rows(plan, packet[LABEL : LABEL + 1].astype(jnp.int32), ahead)
    exp_ref[...], cpl_ref[...], grad_ref[...] = visitor_operands(packet, bias, **uses)


def visit(packet, plan, ahead, slots, acc_ref, before_ref, home_exp_ref, home_cpl_ref, **uses):
    load(slots, packet, plan, ahead, **uses)
    add_tile(acc_ref, before_ref, home_exp_ref, home_cpl_ref, *slots)


def plan_of(packet, offset):
    return packet[PLAN + offset : PLAN + offset + 1].astype(jnp.int32)


def load_at(slots, second, home, packet, place):
    (ahead_first, offset_first), (ahead_second, offset_second) = place
    ahead = jnp.logical_or(jnp.logical_and(second, ahead_second), jnp.logical_and(~second, ahead_first))
    mine = jnp.where(second, plan_of(home, offset_second), plan_of(home, offset_first))
    theirs = jnp.where(second, plan_of(packet, offset_second), plan_of(packet, offset_first))
    load(slots, packet, jnp.where(ahead, theirs, mine), ahead)


def visit_at(second, home, packet, place, acc_ref, before_ref, factors, slots):
    load_at(slots, second, home, packet, place)
    add_tile(acc_ref, before_ref, *factors, *slots)


def prepare(packet, exp_ref, cpl_ref, rows_ref):
    exponent, coupling = own_operands(packet)
    exp_ref[...] = exponent.T.astype(jnp.bfloat16)
    cpl_ref[...] = coupling.T.astype(jnp.bfloat16)
    rows_ref[...] = gradient_rows(*halves(packet[:F])).astype(jnp.bfloat16)


def is_second(own_ref):
    return own_ref[CORE : CORE + 1, :] > 0.5


def home_kernel(own_ref, acc_ref, exp_ref, cpl_ref, rows_ref, again_ref, *slots):
    own = own_ref[...]
    again_ref[...] = own
    prepare(own, exp_ref, cpl_ref, rows_ref)
    plan = plan_of(own, 0)
    behind = jnp.zeros(plan.shape, jnp.bool_)
    visit(own, plan, behind, slots, acc_ref, None, exp_ref, cpl_ref, use_right=False)
    visit(own, plan, ~behind, slots, acc_ref, acc_ref, exp_ref, cpl_ref, use_left=False)


def near_kernel(own_ref, exp_ref, cpl_ref, before_ref, near_ref, acc_ref, near_exp_ref, near_cpl_ref, near_rows_ref, *slots):
    near = near_ref[...]
    prepare(near, near_exp_ref, near_cpl_ref, near_rows_ref)
    place = ((True, 1), (False, 1))
    visit_at(is_second(own_ref), own_ref[...], near, place, acc_ref, before_ref, (exp_ref, cpl_ref), slots)


def gradient(sums, packet_ref):
    return sums[:F] + sums[2 * F :] - packet_ref[:F, :] * sums[F : 2 * F]


def down_kernel(*refs):
    own_ref, exp_ref, cpl_ref, rows_ref, near_ref, near_exp_ref, near_cpl_ref, near_rows_ref, down_ref = refs[:9]
    hi_ref, lo_ref, near_hi_ref, near_lo_ref, grad_rows_ref, back_grad_ref, turn_ref, back_ref, *slots = refs[9:]
    second, down = is_second(own_ref), down_ref[...]
    load_at(slots, second, near_ref[...], down, ((False, 3), (False, 1)))
    back_tile(back_ref, True, near_exp_ref, near_cpl_ref, near_rows_ref, slots[0], slots[1], near_hi_ref, near_lo_ref)
    load_at(slots, second, own_ref[...], down, ((False, 2), (False, 2)))
    back_tile(back_ref, False, exp_ref, cpl_ref, rows_ref, slots[0], slots[1], hi_ref, lo_ref)
    back_grad_ref[...] = gradient(back_ref[...], down_ref)
    turn_ref[...] = back_grad_ref[:8, :128]
    grad_rows_ref[...] = slots[2][...]


def side_kernel(*refs):
    before_ref, near_ref, hi_ref, lo_ref, near_hi_ref, near_lo_ref, grad_rows_ref, _, acc_ref, near_grad_ref, near_acc_ref = refs
    side_tile(near_acc_ref, None, near_hi_ref, near_lo_ref, grad_rows_ref)
    near_grad_ref[...] = gradient(near_acc_ref[...].T, near_ref)
    side_tile(acc_ref, before_ref, hi_ref, lo_ref, grad_rows_ref)


def far_kernel(own_ref, exp_ref, cpl_ref, before_ref, far_ref, loglen_ref, grad_ref, scale_ref, acc_ref, *slots):
    scale_ref[...] = jnp.broadcast_to(as_column(jnp.exp(-loglen_ref[...])), scale_ref.shape)
    far = far_ref[...]
    visit_at(is_second(own_ref), own_ref[...], far, FAR, acc_ref, before_ref, (exp_ref, cpl_ref), slots)
    grad_ref[...] = gradient(acc_ref[...].T, own_ref)


def as_column(row):
    n = row.shape[1]
    same = lax.broadcasted_iota(jnp.int32, (n, n), 0) == lax.broadcasted_iota(jnp.int32, (n, n), 1)
    return jnp.sum(jnp.where(same, jnp.broadcast_to(row, (n, n)), 0.0), axis=1, keepdims=True)


def project_kernel(plan_ref, projection_ref, loglen_ref, assign_ref, left_ref, right_ref, embeddings_ref, own_ref, *scratch):
    held, sems = scratch[:6], scratch[6]
    points = own_ref.shape[1]
    block = points // PIECES
    sources = (projection_ref, loglen_ref, assign_ref, left_ref, right_ref)
    copies = [pltpu.make_async_copy(source, there, sems.at[n]) for n, (source, there) in enumerate(zip(sources, held))]
    for piece in range(PIECES):
        rows = pl.ds(piece * block, block)
        copies.append(pltpu.make_async_copy(embeddings_ref.at[rows, :], held[5].at[rows, :], sems.at[5 + piece]))
    for copy in copies:
        copy.start()
    for copy in copies[:5]:
        copy.wait()
    projection, loglen, assign, left, right = (there[...] for there in held[:5])
    core = lax.rem(lax.axis_index("blk"), 2).astype(jnp.float32)
    own_ref[LEFT:RIGHT, :] = left
    own_ref[RIGHT:LABEL, :] = right
    rows = [assign.astype(jnp.float32)]
    rows += [jnp.full((1, points), plan_ref[0, offset].astype(jnp.float32)) for offset in range(STEPS)]
    rows += [jnp.full((1, points), core), jnp.zeros((ROWS - CORE - 1, points), jnp.float32)]
    own_ref[LABEL:, :] = jnp.concatenate(rows, axis=0)
    scale = as_column(jnp.exp(-loglen))
    for piece in range(PIECES):
        copies[5 + piece].wait()
        at = slice(piece * block, (piece + 1) * block)
        features = lax.dot_general(projection, held[5][at, :], NT, preferred_element_type=jnp.float32)
        own_ref[:F, at] = features * scale


def slots_of(points):
    return [
        pltpu.VMEM((256, points), jnp.bfloat16),
        pltpu.VMEM((256, points), jnp.bfloat16),
        pltpu.VMEM((WIDE, points), jnp.bfloat16),
    ]


def cost(flops, size=4 << 20):
    return pl.CostEstimate(flops=flops, bytes_accessed=size, transcendentals=0)


def project(embeddings, projection, loglen, left_solves, right_solves, assign, plan):
    points = embeddings.shape[0]
    arrays = (projection.T, loglen[None, :], assign[None, :], left_solves, right_solves, embeddings)
    return pl.pallas_call(
        project_kernel,
        in_specs=[pl.BlockSpec(memory_space=pltpu.SMEM)] + [pl.BlockSpec(memory_space=pltpu.HBM)] * len(arrays),
        out_shape=jax.ShapeDtypeStruct((ROWS, points), jnp.float32),
        scratch_shapes=[pltpu.VMEM(array.shape, array.dtype) for array in arrays]
        + [pltpu.SemaphoreType.DMA((5 + PIECES,))],
        cost_estimate=cost(1 << 20),
        compiler_params=pltpu.CompilerParams(vmem_limit_bytes=62 << 20),
        name="project",
    )(plan.T, *arrays)


def tiles(kernel, outs, points, *operands, scratch=()):
    return pl.pallas_call(
        kernel,
        out_shape=outs,
        scratch_shapes=list(scratch) + (slots_of(points) if points else []),
        cost_estimate=cost(1 << 20),
        compiler_params=pltpu.CompilerParams(vmem_limit_bytes=40 << 20),
        name=kernel.__name__,
    )(*operands)


def sent(value, target, takes=lambda source: True):
    count = lax.axis_size("blk")
    pairs = [(source, target(source) % count) for source in range(count) if takes(source)]
    return lax.ppermute(value, "blk", pairs)


def twin(value):
    return sent(value, lambda i: i ^ 1)


def sum_over_blk(term):
    count = lax.axis_size("blk")
    index = lax.axis_index("blk")
    second = (index % 2) == 1
    half = term.shape[0] // 2
    give = jnp.where(second, term[:half], term[half:])
    total = jnp.where(second, term[half:], term[:half]) + twin(give)
    spreads, unit = [], 4
    while unit < count:
        spread = min(4, count // unit)
        place = (index // unit) % spread
        if total.shape[0] % spread == 0:
            spreads.append((unit, spread, place))
            shares = total.reshape(spread, total.shape[0] // spread, total.shape[1])
            total = lax.dynamic_index_in_dim(shares, place, 0, False)
            for hop in range(spread - 1, 0, -1):
                passed = lax.dynamic_index_in_dim(shares, place ^ hop, 0, False)
                total = total + sent(passed, lambda i, step=unit * hop: i ^ step)
        else:
            for bit in range(1, spread.bit_length()):
                total = total + sent(total, lambda i, step=unit * bit: i ^ step)
        unit *= spread
    total = total + sent(total, lambda i: i ^ 2)
    for unit, spread, place in reversed(spreads):
        got = [total] + [sent(total, lambda i, step=unit * hop: i ^ step) for hop in range(1, spread)]
        got = jnp.stack(got)
        total = jnp.concatenate([lax.dynamic_index_in_dim(got, place ^ at, 0, False) for at in range(spread)])
    other = twin(total)
    return jnp.where(second, jnp.concatenate([other, total]), jnp.concatenate([total, other]))


def across(i):
    return i + 3 if i % 2 else i - 3


def per_device(embeddings, projection, loglen, left_solves, right_solves, assign, plan):
    points = embeddings.shape[0]
    sums = jax.ShapeDtypeStruct((points, WIDE), jnp.float32)
    factor = jax.ShapeDtypeStruct((points, 256), jnp.bfloat16)
    rows = jax.ShapeDtypeStruct((WIDE, points), jnp.bfloat16)
    block = jax.ShapeDtypeStruct((ROWS, points), jnp.float32)
    grads = jax.ShapeDtypeStruct((F, points), jnp.float32)
    sums_held = pltpu.VMEM(sums.shape, sums.dtype)

    own = project(embeddings, projection, loglen, left_solves, right_solves, assign, plan)
    down = sent(own, lambda i: i + 2)
    near = twin(own)
    acc, own_exp, own_cpl, own_rows, own = tiles(home_kernel, (sums, factor, factor, rows, block), points, own)
    far = sent(own, across)
    home = (own, own_exp, own_cpl)
    acc, *near_factors = tiles(near_kernel, (sums, factor, factor, rows), points, *home, acc, near)
    weights = jax.ShapeDtypeStruct((points, points), jnp.bfloat16)
    *kept, down_rows, down_grad, turn = tiles(
        down_kernel,
        (weights, weights, weights, weights, rows, grads, jax.ShapeDtypeStruct((8, 128), jnp.float32)),
        points,
        *home,
        own_rows,
        near,
        *near_factors,
        down,
        scratch=[pltpu.VMEM((WIDE, points), jnp.float32)],
    )
    back = sent(down_grad, lambda i: i - 2)
    acc, near_grad = tiles(side_kernel, (sums, grads), None, acc, near, *kept, down_rows, twin(turn), scratch=[sums_held])
    passed = twin(near_grad)
    grad, scale = tiles(far_kernel, (grads, grads), points, *home, acc, far, loglen[None, :], scratch=[sums_held])
    grad_x = ((grad + passed + back) * scale).astype(jnp.bfloat16)
    term = lax.dot_general(grad_x, embeddings, (((1,), (0,)), ((), ())), preferred_element_type=jnp.float32)
    return sum_over_blk(term).T


def solution(mesh):
    return jax.shard_map(
        per_device,
        mesh=mesh,
        in_specs=(
            P(("parts", "blk"), None),
            P("parts", None),
            P("parts"),
            P(None, ("parts", "blk")),
            P(None, ("parts", "blk")),
            P(("parts", "blk")),
            P(None, ("parts", "blk")),
        ),
        out_specs=P("parts", None),
        check_vma=False,
    )
```
